32 devices in a mesh: row: 8 (over z, y), col: 4 (over x, core).
Axes of the slice: x: 2, y: 2, z: 4, core: 2. Of those that a mesh axis runs over, the one named last changes fastest.
Arguments:
- raw: int32 [8192, 4096], P('col', 'row'), may hold values from -128 to 127
- taps: int32 [16, 128], replicated, may hold values from -256 to 256
Outputs:
- visibility: bfloat16 [32, 4096, 2, 4096], P(None, 'row', None, 'col')
The draws below stay inside these ranges and needn't reach their ends.
All inputs are finite; a program needn't handle non-finite values.
Results may differ from the reference program's by a relative error of at most 0.0056.
Values may be sent and summed in bfloat16 or wider, within the bound.
No kernel may reach another device: no remote copies, remote signals or barrier semaphores. Data moves between devices by JAX's collectives and lax.ppermute only.
A program may use at most 384 MiB of HBM per device.

```python
import math
import jax
import jax.numpy as jnp
from jax import lax

INPUTS = 4096
CHANNELS = 32
TRANSFORM = 128
TAPS = 16
BLOCKS = 2
SPECTRA = 64
SAMPLES = 8192


def place_ends(array, own_key, low, top_value):
    place = [jax.random.randint(jax.random.fold_in(own_key, axis), (), 0, length) for axis, length in enumerate(array.shape)]
    widest = array.shape.index(max(array.shape))
    beside = place[:widest] + [(place[widest] + 1) % array.shape[widest]] + place[widest + 1:]
    return array.at[tuple(place)].set(low).at[tuple(beside)].set(top_value)


def setup_inputs(seed: int = 0) -> dict:
    keys = jax.random.split(jax.random.key(seed), 3)
    raw = place_ends(jax.random.randint(keys[0], (SAMPLES, INPUTS), -128, 128), jax.random.fold_in(keys[0], 1), -128, 127).astype(jnp.int32)
    taps = place_ends(jax.random.randint(keys[1], (TAPS, TRANSFORM), -256, 257), jax.random.fold_in(keys[1], 1), -256, 256).astype(jnp.int32)
    return dict(raw=raw, taps=taps)


def dft_table():
    sample = jnp.arange(TRANSFORM, dtype=jnp.int32)[:, None]
    channel = jnp.arange(1, CHANNELS + 1, dtype=jnp.int32)[None, :]
    phase = (sample * channel % TRANSFORM).astype(jnp.float32) * (2.0 * math.pi / TRANSFORM)
    return jnp.concatenate([jnp.cos(phase), -jnp.sin(phase)], axis=1)

def channelize(extended, taps, count):
    coeffs = taps.astype(jnp.float32)
    weighted = jnp.zeros((count, TRANSFORM, extended.shape[2]), jnp.float32)
    for offset in range(TAPS):
        start = TAPS - 1 - offset
        weighted = weighted + coeffs[offset][None, :, None] * extended[start:start + count].astype(jnp.float32)
    scale = 1.0 / (8192.0 * math.sqrt(TAPS * TRANSFORM))
    spectra = jnp.einsum('sni,nk->ksi', weighted, dft_table(), precision=lax.Precision.HIGHEST) * scale
    return spectra.reshape(2, CHANNELS, count, extended.shape[2]).astype(jnp.bfloat16)

def correlate_channel(pair):
    left_real, left_imag = pair
    width = SPECTRA // BLOCKS
    total = jnp.zeros((INPUTS, 2 * INPUTS), jnp.float32)
    carry = jnp.zeros((INPUTS, 2 * INPUTS), jnp.float32)
    for block in range(BLOCKS):
        real_part = left_real[block * width:(block + 1) * width]
        imag_part = left_imag[block * width:(block + 1) * width]
        left = jnp.concatenate([real_part, imag_part], axis=0)
        right = jnp.concatenate([jnp.concatenate([real_part, imag_part], axis=0), jnp.concatenate([-imag_part, real_part], axis=0)], axis=1)
        term = lax.dot_general(left, right, (((0,), (0,)), ((), ())), preferred_element_type=jnp.float32)
        if block == 0:
            total = term
        else:
            shifted = term - carry
            summed = total + shifted
            carry = summed - total - shifted
            total = summed
    return (total * (1.0 / SPECTRA)).astype(jnp.bfloat16)

def reference(raw, taps):
    frames = raw.astype(jnp.bfloat16).reshape(SPECTRA, TRANSFORM, INPUTS)
    extended = jnp.concatenate([jnp.zeros((TAPS - 1, TRANSFORM, INPUTS), jnp.bfloat16), frames], axis=0)
    spectra = channelize(extended, taps, SPECTRA)
    result = lax.map(correlate_channel, (spectra[0], spectra[1]))
    return result.reshape(CHANNELS, INPUTS, 2, INPUTS)
```

```python
import math

import jax
import jax.numpy as jnp
from jax import lax
from jax.sharding import PartitionSpec as P

CHANNELS = 32
TRANSFORM = 128
TAPS = 16
SPECTRA_DEV = 16
BLOCKS = 2
CHUNKS = 4


def from_behind(block, axis, distance):
    devices = range(lax.axis_size(axis))
    route = [(i - distance, i) for i in devices if i - distance in devices]
    return lax.ppermute(block, axis, route)


def from_root(value, axis, root):
    mine = lax.axis_index(axis) == root
    return lax.psum(jnp.where(mine, value, jnp.zeros_like(value)), axis)


def dft_table():
    sample = jnp.arange(TRANSFORM, dtype=jnp.int32)[:, None]
    channel = jnp.arange(1, CHANNELS + 1, dtype=jnp.int32)[None, :]
    phase = (sample * channel % TRANSFORM).astype(jnp.float32) * (2.0 * math.pi / TRANSFORM)
    return jnp.concatenate([jnp.cos(phase), -jnp.sin(phase)], axis=1)


def channelize(extended, taps, count):
    coeffs = taps.astype(jnp.float32)
    weighted = jnp.zeros((count, TRANSFORM, extended.shape[2]), jnp.float32)
    for offset in range(TAPS):
        start = TAPS - 1 - offset
        weighted = weighted + coeffs[offset][None, :, None] * extended[
            start : start + count
        ].astype(jnp.float32)
    scale = 1.0 / (8192.0 * math.sqrt(TAPS * TRANSFORM))
    spectra = (
        jnp.einsum("sni,nk->ksi", weighted, dft_table(), precision=lax.Precision.HIGHEST) * scale
    )
    return spectra.reshape(2, CHANNELS, count, extended.shape[2]).astype(jnp.bfloat16)


def extend(raw):
    frames = raw.astype(jnp.bfloat16).reshape(SPECTRA_DEV, TRANSFORM, raw.shape[1])
    rim_frames = frames[SPECTRA_DEV - (TAPS - 1) :]
    earlier = from_behind(rim_frames, "col", 1)
    return jnp.concatenate([earlier, frames], axis=0)


def correlate(row_block, column_block):
    spectra_all = row_block.shape[2]
    left = jnp.concatenate([row_block[0], row_block[1]], axis=1)
    real_part, imag_part = column_block[0], column_block[1]
    right = jnp.concatenate(
        [
            jnp.concatenate([real_part, imag_part], axis=1),
            jnp.concatenate([-imag_part, real_part], axis=1),
        ],
        axis=2,
    )
    total = lax.dot_general(
        left, right, (((1,), (1,)), ((0,), (0,))), preferred_element_type=jnp.float32
    )
    result = (total * (1.0 / spectra_all)).astype(jnp.bfloat16)
    return result.reshape(CHANNELS, row_block.shape[3], 2, column_block.shape[3])


def general_body(raw, taps):
    pieces = channelize(extend(raw), taps, SPECTRA_DEV)
    row_block = lax.all_gather(pieces, "col", axis=2, tiled=True)
    ratio = lax.axis_size("row") // lax.axis_size("col")
    first_root = lax.axis_index("col") * ratio
    received = []
    for offset in range(ratio):
        received.append(from_root(row_block, "row", first_root + offset))
    column_block = jnp.concatenate(received, axis=3)
    return correlate(row_block, column_block)


def correlate_chunk(chunk, y, row_part, near, far, buffer, spectra_all):
    pieces, count, depth, width = row_part.shape
    half = depth // 2
    turned = jnp.concatenate([row_part[:, :, half:], -row_part[:, :, :half]], axis=2)
    left = jnp.stack([row_part, turned], axis=-1).reshape(pieces, count, depth, 2 * width)
    left = jnp.transpose(left, (1, 3, 0, 2)).reshape(count, 2 * width, pieces * depth)
    low = jnp.where(y == 0, near, far)
    high = jnp.where(y == 0, far, near)
    right = jnp.concatenate([low, high], axis=3)
    right = jnp.transpose(right, (1, 0, 2, 3)).reshape(count, pieces * depth, 2 * width)
    total = lax.dot_general(
        left, right, (((2,), (1,)), ((0,), (0,))), preferred_element_type=jnp.float32
    )
    part = (total * (1.0 / spectra_all)).astype(jnp.bfloat16)
    part = part.reshape(count, width, 2, 2 * width)
    return lax.dynamic_update_slice(buffer, part, (chunk * count, 0, 0, 0))


def device(z, y, c):
    return (z * 2 + y) * 4 + c


def routes():
    everywhere = [(z, y, c) for z in range(4) for y in range(2) for c in range(4)]
    core = [(device(z, y, c), device(z, y, c ^ 1)) for z, y, c in everywhere]
    across = [(device(z, y, c), device(z, y, c ^ 2)) for z, y, c in everywhere]
    other = [(device(z, y, c), device(z, 1 - y, c)) for z, y, c in everywhere]
    hops = [
        {0: [(0, 1)], 1: [(1, 2)], 2: [(2, 1)], 3: [(3, 2)]},
        {0: [(1, 2)], 1: [(2, 3), (1, 0)], 2: [(1, 0), (2, 3)], 3: [(2, 1)]},
        {0: [(2, 3)], 3: [(1, 0)]},
    ]
    chain = [
        [
            (device(a, y, c), device(b, y, c))
            for c, pairs in hop.items()
            for a, b in pairs
            for y in range(2)
        ]
        for hop in hops
    ]
    return core, across, other, chain


def arrival(z, c):
    away = jnp.abs(z - c)
    late = ((c == 1) & (z != 2)) | ((c == 2) & (z != 1))
    return jnp.where(away == 0, 0, jnp.where(late, 2, away))


def plane_body(raw, taps):
    core, across, other, chain = routes()
    axes = ("row", "col")
    row, col = lax.axis_index("row"), lax.axis_index("col")
    z, y = row // 2, row % 2
    hop = arrival(z, col)
    pieces = channelize(extend(raw), taps, SPECTRA_DEV)
    width = pieces.shape[3]
    own = jnp.transpose(pieces, (1, 0, 2, 3)).reshape(CHANNELS, 2 * SPECTRA_DEV, width)
    count = CHANNELS // CHUNKS
    spectra_all = SPECTRA_DEV * lax.axis_size("col")
    result = jnp.zeros((CHANNELS, width, 2, 2 * width), jnp.bfloat16)
    for chunk in range(CHUNKS):
        mine = own[chunk * count : (chunk + 1) * count]
        opposite = lax.ppermute(mine, axes, across)
        pair = jnp.stack([mine, opposite])
        row_part = jnp.concatenate([pair, lax.ppermute(pair, axes, core)], axis=0)
        first = lax.ppermute(row_part, axes, chain[0])
        held = jnp.where(hop == 0, row_part, first)
        second = lax.ppermute(held, axes, chain[1])
        held = jnp.where(hop == 2, second, held)
        third = lax.ppermute(second, axes, chain[2])
        near = jnp.where(hop == 3, third, held)
        far = lax.ppermute(near, axes, other)
        result = correlate_chunk(chunk, y, row_part, near, far, result, spectra_all)
    return result


def solution(mesh):
    planes = mesh.shape["row"] == 8 and mesh.shape["col"] == 4
    placed = (P("col", "row"), P())
    return jax.shard_map(
        plane_body if planes else general_body,
        mesh=mesh,
        in_specs=placed,
        out_specs=P(None, "row", None, "col"),
        check_vma=False,
    )
```

```python
import math

import jax
import jax.numpy as jnp
from jax import lax
from jax.sharding import PartitionSpec as P

CHANNELS = 32
TRANSFORM = 128
TAPS = 16
SPECTRA_DEV = 16
BLOCKS = 2
CHUNKS = 4


def from_behind(block, axis, distance):
    devices = range(lax.axis_size(axis))
    route = [(i - distance, i) for i in devices if i - distance in devices]
    return lax.ppermute(block, axis, route)


def from_root(value, axis, root):
    mine = lax.axis_index(axis) == root
    return lax.psum(jnp.where(mine, value, jnp.zeros_like(value)), axis)


def dft_table():
    sample = jnp.arange(TRANSFORM, dtype=jnp.int32)[:, None]
    channel = jnp.arange(1, CHANNELS + 1, dtype=jnp.int32)[None, :]
    phase = (sample * channel % TRANSFORM).astype(jnp.float32) * (2.0 * math.pi / TRANSFORM)
    return jnp.concatenate([jnp.cos(phase), -jnp.sin(phase)], axis=1)


def channelize(extended, taps, count):
    coeffs = taps.astype(jnp.float32)
    weighted = jnp.zeros((count, TRANSFORM, extended.shape[2]), jnp.float32)
    for offset in range(TAPS):
        start = TAPS - 1 - offset
        weighted = weighted + coeffs[offset][None, :, None] * extended[
            start : start + count
        ].astype(jnp.float32)
    scale = 1.0 / (8192.0 * math.sqrt(TAPS * TRANSFORM))
    spectra = (
        jnp.einsum("sni,nk->ksi", weighted, dft_table(), precision=lax.Precision.HIGHEST) * scale
    )
    return spectra.reshape(2, CHANNELS, count, extended.shape[2]).astype(jnp.bfloat16)


def extend(raw):
    frames = raw.astype(jnp.bfloat16).reshape(SPECTRA_DEV, TRANSFORM, raw.shape[1])
    rim_frames = frames[SPECTRA_DEV - (TAPS - 1) :]
    earlier = from_behind(rim_frames, "col", 1)
    return jnp.concatenate([earlier, frames], axis=0)


def correlate(row_block, column_block):
    spectra_all = row_block.shape[2]
    left = jnp.concatenate([row_block[0], row_block[1]], axis=1)
    real_part, imag_part = column_block[0], column_block[1]
    right = jnp.concatenate(
        [
            jnp.concatenate([real_part, imag_part], axis=1),
            jnp.concatenate([-imag_part, real_part], axis=1),
        ],
        axis=2,
    )
    total = lax.dot_general(
        left, right, (((1,), (1,)), ((0,), (0,))), preferred_element_type=jnp.float32
    )
    result = (total * (1.0 / spectra_all)).astype(jnp.bfloat16)
    return result.reshape(CHANNELS, row_block.shape[3], 2, column_block.shape[3])


def general_body(raw, taps):
    pieces = channelize(extend(raw), taps, SPECTRA_DEV)
    row_block = lax.all_gather(pieces, "col", axis=2, tiled=True)
    ratio = lax.axis_size("row") // lax.axis_size("col")
    first_root = lax.axis_index("col") * ratio
    received = []
    for offset in range(ratio):
        received.append(from_root(row_block, "row", first_root + offset))
    column_block = jnp.concatenate(received, axis=3)
    return correlate(row_block, column_block)


def correlate_planes(row_part, low, high, spectra_all):
    pieces, count, depth, width = row_part.shape
    half = depth // 2

    def stacked(part):
        return jnp.transpose(part, (1, 0, 2, 3)).reshape(count, pieces * depth, width)

    def turn(part):
        return jnp.concatenate([-part[:, :, half:], part[:, :, :half]], axis=2)

    left = stacked(row_part)
    blocks = [stacked(low), stacked(high), stacked(turn(low)), stacked(turn(high))]
    right = jnp.concatenate(blocks, axis=2)
    total = lax.dot_general(
        left, right, (((1,), (1,)), ((0,), (0,))), preferred_element_type=jnp.float32
    )
    result = (total * (1.0 / spectra_all)).astype(jnp.bfloat16)
    return result.reshape(count, width, 2, 2 * width)


def device(z, y, c):
    return (z * 2 + y) * 4 + c


def routes():
    everywhere = [(z, y, c) for z in range(4) for y in range(2) for c in range(4)]
    core = [(device(z, y, c), device(z, y, c ^ 1)) for z, y, c in everywhere]
    across = [(device(z, y, c), device(z, y, c ^ 2)) for z, y, c in everywhere]
    other = [(device(z, y, c), device(z, 1 - y, c)) for z, y, c in everywhere]
    hops = [
        {0: [(0, 1)], 1: [(1, 2)], 2: [(2, 1)], 3: [(3, 2)]},
        {0: [(1, 2)], 1: [(2, 3), (1, 0)], 2: [(1, 0), (2, 3)], 3: [(2, 1)]},
        {0: [(2, 3)], 3: [(1, 0)]},
    ]
    chain = [
        [
            (device(a, y, c), device(b, y, c))
            for c, pairs in hop.items()
            for a, b in pairs
            for y in range(2)
        ]
        for hop in hops
    ]
    return core, across, other, chain


def arrival(z, c):
    away = jnp.abs(z - c)
    late = ((c == 1) & (z != 2)) | ((c == 2) & (z != 1))
    return jnp.where(away == 0, 0, jnp.where(late, 2, away))


def plane_body(raw, taps):
    core, across, other, chain = routes()
    axes = ("row", "col")
    row, col = lax.axis_index("row"), lax.axis_index("col")
    z, y = row // 2, row % 2
    hop = arrival(z, col)
    pieces = channelize(extend(raw), taps, SPECTRA_DEV)
    width = pieces.shape[3]
    own = jnp.transpose(pieces, (1, 0, 2, 3)).reshape(CHANNELS, 2 * SPECTRA_DEV, width)
    count = CHANNELS // CHUNKS
    spectra_all = SPECTRA_DEV * lax.axis_size("col")
    row_parts, lows, highs = [], [], []
    for chunk in range(CHUNKS):
        mine = own[chunk * count : (chunk + 1) * count]
        opposite = lax.ppermute(mine, axes, across)
        pair = jnp.stack([mine, opposite])
        row_part = jnp.concatenate([pair, lax.ppermute(pair, axes, core)], axis=0)
        first = lax.ppermute(row_part, axes, chain[0])
        held = jnp.where(hop == 0, row_part, first)
        second = lax.ppermute(held, axes, chain[1])
        held = jnp.where(hop == 2, second, held)
        third = lax.ppermute(second, axes, chain[2])
        near = jnp.where(hop == 3, third, held)
        far = lax.ppermute(near, axes, other)
        row_parts.append(row_part)
        lows.append(jnp.where(y == 0, near, far))
        highs.append(jnp.where(y == 0, far, near))
    operands = [jnp.concatenate(parts, axis=1) for parts in (row_parts, lows, highs)]
    return correlate_planes(*operands, spectra_all)


def solution(mesh):
    planes = mesh.shape["row"] == 8 and mesh.shape["col"] == 4
    placed = (P("col", "row"), P())
    return jax.shard_map(
        plane_body if planes else general_body,
        mesh=mesh,
        in_specs=placed,
        out_specs=P(None, "row", None, "col"),
        check_vma=False,
    )
```

```python
import math

import jax
import jax.numpy as jnp
from jax import lax
from jax.sharding import PartitionSpec as P

CHANNELS = 32
TRANSFORM = 128
TAPS = 16
SPECTRA_DEV = 16
BLOCKS = 2
CHUNKS = 4


def from_behind(block, axis, distance):
    devices = range(lax.axis_size(axis))
    route = [(i - distance, i) for i in devices if i - distance in devices]
    return lax.ppermute(block, axis, route)


def from_root(value, axis, root):
    mine = lax.axis_index(axis) == root
    return lax.psum(jnp.where(mine, value, jnp.zeros_like(value)), axis)


def dft_table():
    sample = jnp.arange(TRANSFORM, dtype=jnp.int32)[:, None]
    channel = jnp.arange(1, CHANNELS + 1, dtype=jnp.int32)[None, :]
    phase = (sample * channel % TRANSFORM).astype(jnp.float32) * (2.0 * math.pi / TRANSFORM)
    return jnp.concatenate([jnp.cos(phase), -jnp.sin(phase)], axis=1)


def channelize(extended, taps, count):
    coeffs = taps.astype(jnp.float32)
    weighted = jnp.zeros((count, TRANSFORM, extended.shape[2]), jnp.float32)
    for offset in range(TAPS):
        start = TAPS - 1 - offset
        weighted = weighted + coeffs[offset][None, :, None] * extended[
            start : start + count
        ].astype(jnp.float32)
    scale = 1.0 / (8192.0 * math.sqrt(TAPS * TRANSFORM))
    spectra = (
        jnp.einsum("sni,nk->ksi", weighted, dft_table(), precision=lax.Precision.HIGHEST) * scale
    )
    return spectra.reshape(2, CHANNELS, count, extended.shape[2]).astype(jnp.bfloat16)


def extend(raw):
    frames = raw.astype(jnp.bfloat16).reshape(SPECTRA_DEV, TRANSFORM, raw.shape[1])
    rim_frames = frames[SPECTRA_DEV - (TAPS - 1) :]
    earlier = from_behind(rim_frames, "col", 1)
    return jnp.concatenate([earlier, frames], axis=0)


def correlate(row_block, column_block):
    spectra_all = row_block.shape[2]
    left = jnp.concatenate([row_block[0], row_block[1]], axis=1)
    real_part, imag_part = column_block[0], column_block[1]
    right = jnp.concatenate(
        [
            jnp.concatenate([real_part, imag_part], axis=1),
            jnp.concatenate([-imag_part, real_part], axis=1),
        ],
        axis=2,
    )
    total = lax.dot_general(
        left, right, (((1,), (1,)), ((0,), (0,))), preferred_element_type=jnp.float32
    )
    result = (total * (1.0 / spectra_all)).astype(jnp.bfloat16)
    return result.reshape(CHANNELS, row_block.shape[3], 2, column_block.shape[3])


def general_body(raw, taps):
    pieces = channelize(extend(raw), taps, SPECTRA_DEV)
    row_block = lax.all_gather(pieces, "col", axis=2, tiled=True)
    ratio = lax.axis_size("row") // lax.axis_size("col")
    first_root = lax.axis_index("col") * ratio
    received = []
    for offset in range(ratio):
        received.append(from_root(row_block, "row", first_root + offset))
    column_block = jnp.concatenate(received, axis=3)
    return correlate(row_block, column_block)


def correlate_planes(row_part, low, high, spectra_all):
    pieces, count, depth, width = row_part.shape
    half = depth // 2

    def stacked(part):
        return jnp.transpose(part, (1, 0, 2, 3)).reshape(count, pieces * depth, width)

    def turn(part):
        return jnp.concatenate([-part[:, :, half:], part[:, :, :half]], axis=2)

    left = stacked(row_part)
    blocks = [stacked(low), stacked(high), stacked(turn(low)), stacked(turn(high))]
    right = jnp.concatenate(blocks, axis=2)
    total = lax.dot_general(
        left, right, (((1,), (1,)), ((0,), (0,))), preferred_element_type=jnp.float32
    )
    result = (total * (1.0 / spectra_all)).astype(jnp.bfloat16)
    return result.reshape(count, width, 2, 2 * width)


def device(z, y, c):
    return (z * 2 + y) * 4 + c


def routes():
    everywhere = [(z, y, c) for z in range(4) for y in range(2) for c in range(4)]
    core = [(device(z, y, c), device(z, y, c ^ 1)) for z, y, c in everywhere]
    across = [(device(z, y, c), device(z, y, c ^ 2)) for z, y, c in everywhere]
    other = [(device(z, y, c), device(z, 1 - y, c)) for z, y, c in everywhere]
    hops = [
        {0: [(0, 1)], 1: [(1, 2)], 2: [(2, 1)], 3: [(3, 2)]},
        {0: [(1, 2)], 1: [(2, 3), (1, 0)], 2: [(1, 0), (2, 3)], 3: [(2, 1)]},
        {0: [(2, 3)], 3: [(1, 0)]},
    ]
    chain = [
        [
            (device(a, y, c), device(b, y, c))
            for c, pairs in hop.items()
            for a, b in pairs
            for y in range(2)
        ]
        for hop in hops
    ]
    return core, across, other, chain


def arrival(z, c):
    away = jnp.abs(z - c)
    late = ((c == 1) & (z != 2)) | ((c == 2) & (z != 1))
    return jnp.where(away == 0, 0, jnp.where(late, 2, away))


def plane_body(raw, taps):
    core, across, other, chain = routes()
    axes = ("row", "col")
    row, col = lax.axis_index("row"), lax.axis_index("col")
    z, y = row // 2, row % 2
    hop = arrival(z, col)
    pieces = channelize(extend(raw), taps, SPECTRA_DEV)
    width = pieces.shape[3]
    own = jnp.transpose(pieces, (1, 0, 2, 3)).reshape(CHANNELS, 2 * SPECTRA_DEV, width)
    count = CHANNELS // CHUNKS
    spectra_all = SPECTRA_DEV * lax.axis_size("col")
    row_parts, lows, highs = [], [], []
    arrived, fars = [], []
    for chunk in range(CHUNKS):
        mine = own[chunk * count : (chunk + 1) * count]
        opposite = lax.ppermute(mine, axes, across)
        pair = jnp.stack([mine, opposite])
        row_part = jnp.concatenate([pair, lax.ppermute(pair, axes, core)], axis=0)
        if chunk >= 2:
            row_part, arrived[-2] = lax.optimization_barrier((row_part, arrived[-2]))
        first = lax.ppermute(row_part, axes, chain[0])
        held = jnp.where(hop == 0, row_part, first)
        if chunk >= 2:
            held, fars[-2] = lax.optimization_barrier((held, fars[-2]))
        second = lax.ppermute(held, axes, chain[1])
        held = jnp.where(hop == 2, second, held)
        third = lax.ppermute(second, axes, chain[2])
        near = jnp.where(hop == 3, third, held)
        arrived.append(near)
        far = lax.ppermute(near, axes, other)
        row_parts.append(row_part)
        fars.append(far)
    for near, far in zip(arrived, fars):
        lows.append(jnp.where(y == 0, near, far))
        highs.append(jnp.where(y == 0, far, near))
    operands = [jnp.concatenate(parts, axis=1) for parts in (row_parts, lows, highs)]
    return correlate_planes(*operands, spectra_all)


def solution(mesh):
    planes = mesh.shape["row"] == 8 and mesh.shape["col"] == 4
    placed = (P("col", "row"), P())
    return jax.shard_map(
        plane_body if planes else general_body,
        mesh=mesh,
        in_specs=placed,
        out_specs=P(None, "row", None, "col"),
        check_vma=False,
    )
```

```python
import math

import jax
import jax.numpy as jnp
from jax import lax
from jax.sharding import PartitionSpec as P

CHANNELS = 32
TRANSFORM = 128
TAPS = 16
SPECTRA_DEV = 16
BLOCKS = 2
CHUNKS = 4


def from_behind(block, axis, distance):
    devices = range(lax.axis_size(axis))
    route = [(i - distance, i) for i in devices if i - distance in devices]
    return lax.ppermute(block, axis, route)


def from_root(value, axis, root):
    mine = lax.axis_index(axis) == root
    return lax.psum(jnp.where(mine, value, jnp.zeros_like(value)), axis)


def dft_table():
    sample = jnp.arange(TRANSFORM, dtype=jnp.int32)[:, None]
    channel = jnp.arange(1, CHANNELS + 1, dtype=jnp.int32)[None, :]
    phase = (sample * channel % TRANSFORM).astype(jnp.float32) * (2.0 * math.pi / TRANSFORM)
    return jnp.concatenate([jnp.cos(phase), -jnp.sin(phase)], axis=1)


def channelize(extended, taps, count):
    coeffs = taps.astype(jnp.float32)
    weighted = jnp.zeros((count, TRANSFORM, extended.shape[2]), jnp.float32)
    for offset in range(TAPS):
        start = TAPS - 1 - offset
        weighted = weighted + coeffs[offset][None, :, None] * extended[
            start : start + count
        ].astype(jnp.float32)
    scale = 1.0 / (8192.0 * math.sqrt(TAPS * TRANSFORM))
    spectra = (
        jnp.einsum("sni,nk->ksi", weighted, dft_table(), precision=lax.Precision.HIGHEST) * scale
    )
    return spectra.reshape(2, CHANNELS, count, extended.shape[2]).astype(jnp.bfloat16)


def extend(raw):
    frames = raw.astype(jnp.bfloat16).reshape(SPECTRA_DEV, TRANSFORM, raw.shape[1])
    rim_frames = frames[SPECTRA_DEV - (TAPS - 1) :]
    earlier = from_behind(rim_frames, "col", 1)
    return jnp.concatenate([earlier, frames], axis=0)


def correlate(row_block, column_block):
    spectra_all = row_block.shape[2]
    left = jnp.concatenate([row_block[0], row_block[1]], axis=1)
    real_part, imag_part = column_block[0], column_block[1]
    right = jnp.concatenate(
        [
            jnp.concatenate([real_part, imag_part], axis=1),
            jnp.concatenate([-imag_part, real_part], axis=1),
        ],
        axis=2,
    )
    total = lax.dot_general(
        left, right, (((1,), (1,)), ((0,), (0,))), preferred_element_type=jnp.float32
    )
    result = (total * (1.0 / spectra_all)).astype(jnp.bfloat16)
    return result.reshape(CHANNELS, row_block.shape[3], 2, column_block.shape[3])


def general_body(raw, taps):
    pieces = channelize(extend(raw), taps, SPECTRA_DEV)
    row_block = lax.all_gather(pieces, "col", axis=2, tiled=True)
    ratio = lax.axis_size("row") // lax.axis_size("col")
    first_root = lax.axis_index("col") * ratio
    received = []
    for offset in range(ratio):
        received.append(from_root(row_block, "row", first_root + offset))
    column_block = jnp.concatenate(received, axis=3)
    return correlate(row_block, column_block)


def correlate_planes(row_part, low, high, spectra_all):
    pieces, count, depth, width = row_part.shape
    half = depth // 2

    def stacked(part):
        return jnp.transpose(part, (1, 0, 2, 3)).reshape(count, pieces * depth, width)

    def turn(part):
        return jnp.concatenate([-part[:, :, half:], part[:, :, :half]], axis=2)

    left = stacked(row_part)
    blocks = [stacked(low), stacked(high), stacked(turn(low)), stacked(turn(high))]
    right = jnp.concatenate(blocks, axis=2)
    total = lax.dot_general(
        left, right, (((1,), (1,)), ((0,), (0,))), preferred_element_type=jnp.float32
    )
    result = (total * (1.0 / spectra_all)).astype(jnp.bfloat16)
    return result.reshape(count, width, 2, 2 * width)


def device(z, y, c):
    return (z * 2 + y) * 4 + c


def routes():
    everywhere = [(z, y, c) for z in range(4) for y in range(2) for c in range(4)]
    core = [(device(z, y, c), device(z, y, c ^ 1)) for z, y, c in everywhere]
    across = [(device(z, y, c), device(z, y, c ^ 2)) for z, y, c in everywhere]
    other = [(device(z, y, c), device(z, 1 - y, c)) for z, y, c in everywhere]
    hops = [
        {0: [(0, 1)], 1: [(1, 2)], 2: [(2, 1)], 3: [(3, 2)]},
        {0: [(1, 2)], 1: [(2, 3), (1, 0)], 2: [(1, 0), (2, 3)], 3: [(2, 1)]},
        {0: [(2, 3)], 3: [(1, 0)]},
    ]
    chain = [
        [
            (device(a, y, c), device(b, y, c))
            for c, pairs in hop.items()
            for a, b in pairs
            for y in range(2)
        ]
        for hop in hops
    ]
    return core, across, other, chain


def arrival(z, c):
    away = jnp.abs(z - c)
    late = ((c == 1) & (z != 2)) | ((c == 2) & (z != 1))
    return jnp.where(away == 0, 0, jnp.where(late, 2, away))


def plane_body(raw, taps):
    core, across, other, chain = routes()
    axes = ("row", "col")
    row, col = lax.axis_index("row"), lax.axis_index("col")
    z, y = row // 2, row % 2
    hop = arrival(z, col)
    width = raw.shape[1]
    sides = [extend(raw[:, : width // 2]), extend(raw[:, width // 2 :])]
    pieces = jnp.concatenate([channelize(side, taps, SPECTRA_DEV) for side in sides], axis=3)
    own = jnp.transpose(pieces, (1, 0, 2, 3)).reshape(CHANNELS, 2 * SPECTRA_DEV, width)
    count = CHANNELS // CHUNKS
    spectra_all = SPECTRA_DEV * lax.axis_size("col")
    row_parts, lows, highs = [], [], []
    arrived, fars = [], []
    for chunk in range(CHUNKS):
        mine = own[chunk * count : (chunk + 1) * count]
        opposite = lax.ppermute(mine, axes, across)
        pair = jnp.stack([mine, opposite])
        row_part = jnp.concatenate([pair, lax.ppermute(pair, axes, core)], axis=0)
        if chunk >= 2:
            row_part, arrived[-2] = lax.optimization_barrier((row_part, arrived[-2]))
        first = lax.ppermute(row_part, axes, chain[0])
        held = jnp.where(hop == 0, row_part, first)
        if chunk >= 2:
            held, fars[-2] = lax.optimization_barrier((held, fars[-2]))
        second = lax.ppermute(held, axes, chain[1])
        held = jnp.where(hop == 2, second, held)
        third = lax.ppermute(second, axes, chain[2])
        near = jnp.where(hop == 3, third, held)
        arrived.append(near)
        far = lax.ppermute(near, axes, other)
        row_parts.append(row_part)
        fars.append(far)
    for near, far in zip(arrived, fars):
        lows.append(jnp.where(y == 0, near, far))
        highs.append(jnp.where(y == 0, far, near))
    operands = [jnp.concatenate(parts, axis=1) for parts in (row_parts, lows, highs)]
    return correlate_planes(*operands, spectra_all)


def solution(mesh):
    planes = mesh.shape["row"] == 8 and mesh.shape["col"] == 4
    placed = (P("col", "row"), P())
    return jax.shard_map(
        plane_body if planes else general_body,
        mesh=mesh,
        in_specs=placed,
        out_specs=P(None, "row", None, "col"),
        check_vma=False,
    )
```
